32 devices in a mesh: tm: 4 (over x, core), rows: 8 (over z, y).
Axes of the slice: x: 2, y: 2, z: 4, core: 2. Of those that a mesh axis runs over, the one named last changes fastest.
Arguments:
- latent_feat: bfloat16 [16, 16, 128, 384], P('tm', 'rows'), may hold values from -6 to 6
- norm_gain: float32 [384], replicated, may hold values from 0.25 to 1.75
- conv_weight: bfloat16 [27, 384, 384], replicated, may hold values from -0.0625 to 0.0625
- rgb_weight: bfloat16 [384, 3], replicated, may hold values from -0.3125 to 0.3125
- real_frames: bfloat16 [3, 16, 16, 128], P(None, 'tm', 'rows'), may hold values from -6 to 6
- disc_first: bfloat16 [27, 64, 3], replicated, may hold values from -0.625 to 0.625
- disc_second: bfloat16 [27, 128, 64], replicated, may hold values from -0.15625 to 0.15625
Outputs:
- decoded: bfloat16 [16, 16, 128, 384], P('tm', 'rows')
- match_map: float32 [16, 16, 128], P('tm', 'rows')
The draws below stay inside these ranges and needn't reach their ends.
All inputs are finite; a program needn't handle non-finite values.
Results may differ from the reference program's by a relative error of at most 0.0033.
Values may be sent and summed in bfloat16 or wider, within the bound.
A program may use at most 128 MiB of HBM per device.

```python
import jax
import jax.numpy as jnp
from jax import lax

C = 384
D1 = 64
D2 = 128
WC = 128
FR = 16
H = 16


def shard_levels(own_key, shape, cuts, least, largest):
    gain = 1.0
    for position, parts in cuts:
        heights = jax.random.uniform(jax.random.fold_in(jax.random.fold_in(own_key, 6), position), (parts,), jnp.float32, least / len(cuts), largest / len(cuts))
        gain = gain * jnp.repeat(jnp.exp(heights), shape[position] // parts).reshape((-1,) + (1,) * (len(shape) - 1 - position))
    return gain


def bell_draw(own_key, extent, spread, reach, cuts=(), kind=jnp.bfloat16):
    entries = spread * jax.random.normal(own_key, extent, jnp.float32)
    if cuts:
        entries = entries * shard_levels(own_key, extent, cuts, -0.22, 0.18)
    return jnp.clip(entries, -reach, reach).astype(kind)


def setup_inputs(seed: int = 0) -> dict:
    arg_keys = jax.random.split(jax.random.key(seed), 8)
    latent_feat = bell_draw(arg_keys[0], (FR, H, WC, C), 1.0, 6.0, ((0, 4), (1, 8)))
    norm_gain = jnp.clip(1.0 + 0.15 * jax.random.normal(arg_keys[1], (C,), jnp.float32), 0.25, 1.75)
    conv_weight = bell_draw(arg_keys[2], (27, C, C), (27 * C) ** -0.5, 0.0625)
    rgb_weight = bell_draw(arg_keys[3], (C, 3), C ** -0.5, 0.3125)
    real_frames = bell_draw(arg_keys[4], (3, FR, H, WC), 1.0, 6.0, ((1, 4), (2, 8)))
    disc_first = bell_draw(arg_keys[5], (27, D1, 3), 81 ** -0.5, 0.625)
    disc_second = bell_draw(arg_keys[6], (27, D2, D1), (27 * D1) ** -0.5, 0.15625)
    return {"latent_feat": latent_feat, "norm_gain": norm_gain, "conv_weight": conv_weight, "rgb_weight": rgb_weight, "real_frames": real_frames, "disc_first": disc_first, "disc_second": disc_second}


def leaky(value):
    return jnp.maximum(value, 0.2 * value)

def disc_layer(inputs, weights):
    padded = jnp.pad(inputs, ((0, 0), (1, 1), (1, 1), (1, 1)))
    frames, height, width = (inputs.shape[1], inputs.shape[2], inputs.shape[3])
    total = jnp.zeros((weights.shape[1], frames, height, width), jnp.float32)
    for tap in range(27):
        dt, dh, dw = (tap // 9, tap // 3 % 3, tap % 3)
        piece = padded[:, dt:dt + frames, dh:dh + height, dw:dw + width]
        total = total + jnp.einsum('oc,cthw->othw', weights[tap].astype(jnp.float32), piece.astype(jnp.float32))
    return leaky(total).astype(jnp.bfloat16)

def reference(latent_feat, norm_gain, conv_weight, rgb_weight, real_frames, disc_first, disc_second):
    feats = latent_feat.astype(jnp.float32)
    normed = feats * lax.rsqrt(lax.optimization_barrier(jnp.mean(feats * feats, axis=-1, keepdims=True)) + 1e-06) * norm_gain
    act = jax.nn.silu(normed).astype(jnp.bfloat16)
    frames, height, width, chans = act.shape
    padded = jnp.pad(act, ((2, 0), (1, 1), (1, 1), (0, 0)))
    total = jnp.zeros((frames * height * width, chans), jnp.float32)
    for tap in range(27):
        dt, dh, dw = (tap // 9, tap // 3 % 3, tap % 3)
        piece = padded[dt:dt + frames, dh:dh + height, dw:dw + width].reshape(-1, chans)
        total = total + jnp.dot(piece, conv_weight[tap], preferred_element_type=jnp.float32)
    decoded = (feats + total.reshape(frames, height, width, chans)).astype(jnp.bfloat16)
    colour = jnp.dot(decoded.reshape(-1, chans), rgb_weight, preferred_element_type=jnp.float32).astype(jnp.bfloat16)
    fake = jnp.transpose(colour.reshape(frames, height, width, 3), (3, 0, 1, 2))
    first_fake = disc_layer(fake, disc_first)
    first_real = disc_layer(real_frames, disc_first)
    second_fake = disc_layer(first_fake, disc_second)
    second_real = disc_layer(first_real, disc_second)
    match_map = lax.optimization_barrier(jnp.mean(jnp.abs(first_fake.astype(jnp.float32) - first_real.astype(jnp.float32)), axis=0))
    match_map = match_map + lax.optimization_barrier(jnp.mean(jnp.abs(second_fake.astype(jnp.float32) - second_real.astype(jnp.float32)), axis=0))
    return (decoded, match_map)
```

```python
import functools

import jax
import jax.numpy as jnp
from jax import lax
from jax.experimental import pallas as pl
from jax.experimental.pallas import tpu as pltpu
from jax.sharding import PartitionSpec as P

MESH = pl.DeviceIdType.MESH
F32 = jnp.float32
BF16 = jnp.bfloat16
SIDES = [(i, j) for i in (-1, 0, 1) for j in (-1, 0, 1) if (i, j) != (0, 0)]


def leaky(value):
    return jnp.maximum(value, 0.2 * value)


def span(step, size):
    if step == 0:
        return 2, 2, size
    return (size, 0, 2) if step > 0 else (2, size + 2, 2)


def shifted(value, step):
    width = value.shape[-1]
    lane = lax.broadcasted_iota(jnp.int32, value.shape, value.ndim - 1)
    moved = pltpu.roll(value, step % width, value.ndim - 1)
    edge = 0 if step > 0 else width - 1
    return jnp.where(lane == edge, 0.0, moved)


def tripled(value):
    row = lax.broadcasted_iota(jnp.int32, value.shape, 0)
    out = jnp.where(row < 3, shifted(value, 1), jnp.where(row < 6, value, shifted(value, -1)))
    return jnp.where(row < 9, out, 0.0).astype(BF16)


def kernel(
    slabs, bands, lat, gain, w_hbm, rgb, real, d1, d2, dec, match,
    wv, ext, acc, grid, feat, second, w1, w2, real32,
    w_sem, row_s, row_r, tm_s, tm_r, relay_s, relay_r, g_s, g_r,
):
    frames, height, width, chans = lat.shape
    depth, depth2 = d1.shape[1], d2.shape[1]
    tm, band = lax.axis_index("tm"), lax.axis_index("rows")

    def exists(i, j):
        ok = jnp.bool_(True)
        if i:
            ok = ok & (tm + i >= 0) & (tm + i < slabs)
        if j:
            ok = ok & (band + j >= 0) & (band + j < bands)
        return ok

    loads = []
    for dh in range(3):
        for dw in range(3):
            copy = pltpu.make_async_copy(
                w_hbm.at[:, dh, dw], wv.at[dh, :, :, pl.ds(dw * chans, chans)], w_sem.at[dh, dw]
            )
            copy.start()
            loads.append(copy)

    barrier = pltpu.get_barrier_semaphore()
    count = jnp.int32(0)
    for i, j in SIDES:
        ok = exists(i, j)
        count = count + ok.astype(jnp.int32)

        @pl.when(ok)
        def _(i=i, j=j):
            pl.semaphore_signal(barrier, inc=1, device_id=(tm + i, band + j), device_id_type=MESH)

    for f in range(frames):
        for r in range(height):
            x = lat[f, r].astype(F32)
            scale = lax.rsqrt(jnp.mean(x * x, axis=-1, keepdims=True) + 1e-06)
            ext[f + 2, r + 1] = jax.nn.silu(x * scale * gain[...]).astype(BF16)

    @pl.when(tm == 0)
    def _():
        ext[0:2] = jnp.zeros((2,) + ext.shape[1:], BF16)

    @pl.when((band == 0) & (tm > 0))
    def _():
        ext[0:2, 0] = jnp.zeros((2, width, chans), BF16)

    @pl.when((band == bands - 1) & (tm > 0))
    def _():
        ext[0:2, height + 1] = jnp.zeros((2, width, chans), BF16)

    @pl.when(band == 0)
    def _():
        ext[2:, 0] = jnp.zeros((frames, width, chans), BF16)

    @pl.when(band == bands - 1)
    def _():
        ext[2:, height + 1] = jnp.zeros((frames, width, chans), BF16)

    pl.semaphore_wait(barrier, count)

    halves = [(frames, 2), (2, frames - 2)]

    def row_copy(side, half):
        start, size = halves[half]
        mine, theirs = (1, height + 1) if side < 0 else (height, 0)
        where = 0 if side < 0 else 1
        return pltpu.make_async_remote_copy(
            src_ref=ext.at[pl.ds(start, size), mine],
            dst_ref=ext.at[pl.ds(start, size), theirs],
            send_sem=row_s.at[where, half],
            recv_sem=row_r.at[where, half],
            device_id=(tm, band + side),
            device_id_type=MESH,
        )

    tm_copy = pltpu.make_async_remote_copy(
        src_ref=ext.at[pl.ds(frames, 2), pl.ds(1, height)],
        dst_ref=ext.at[pl.ds(0, 2), pl.ds(1, height)],
        send_sem=tm_s,
        recv_sem=tm_r,
        device_id=(tm + 1, band),
        device_id_type=MESH,
    )

    def relay_copy(where):
        row = 0 if where else height + 1
        return pltpu.make_async_remote_copy(
            src_ref=ext.at[pl.ds(frames, 2), row],
            dst_ref=ext.at[pl.ds(0, 2), row],
            send_sem=relay_s.at[where],
            recv_sem=relay_r.at[where],
            device_id=(tm + 1, band),
            device_id_type=MESH,
        )

    def grid_copy(kind, side):
        i, j = SIDES[side]
        (fs, fd, fn), (rs, rd, rn) = span(i, frames), span(j, height)
        return pltpu.make_async_remote_copy(
            src_ref=grid.at[kind, pl.ds(fs, fn), pl.ds(rs, rn)],
            dst_ref=grid.at[kind, pl.ds(fd, fn), pl.ds(rd, rn)],
            send_sem=g_s.at[kind, side],
            recv_sem=g_r.at[kind, side],
            device_id=(tm + i, band + j),
            device_id_type=MESH,
        )

    def when(ok, action):
        pl.when(ok)(action)

    when(exists(1, 0), lambda: tm_copy.start())
    for half in (0, 1):
        for side in (-1, 1):
            when(exists(0, side), lambda: row_copy(side, half).start())

    def grid_zero(kind):
        for side in range(len(SIDES)):
            i, j = SIDES[side]
            (_, fd, fn), (_, rd, rn) = span(i, frames), span(j, height)

            @pl.when(jnp.logical_not(exists(-i, -j)))
            def _():
                grid[kind, fd:fd + fn, rd:rd + rn] = jnp.zeros((fn, rn, 16, width), BF16)

    def grid_send(kind):
        for side in range(len(SIDES)):
            when(exists(*SIDES[side]), lambda: grid_copy(kind, side).start())

    def grid_wait(kind):
        for side in range(len(SIDES)):
            i, j = SIDES[side]
            when(exists(-i, -j), lambda: grid_copy(kind, side).wait_recv())

    grid_zero(0)
    grid_zero(1)
    real32[...] = real[...].astype(F32)
    row = lax.broadcasted_iota(jnp.int32, (16, width), 0)
    for f in range(frames):
        for r in range(height):
            b0, b1, b2 = [
                jnp.broadcast_to(real32[c, f, r:r + 1], (16, width)) for c in range(3)
            ]
            cell = jnp.where(row % 3 == 0, b0, jnp.where(row % 3 == 1, b1, b2))
            grid[1, f + 2, r + 2] = tripled(cell)
    grid_send(1)

    def lhs(f0, nf, row):
        return jnp.concatenate(
            [ext[f0 + dt:f0 + dt + nf, row].reshape(nf * width, chans) for dt in range(3)], axis=1
        )

    def own(f0, nf):
        for r in range(height):
            taps = [dh for dh in range(3) if 1 <= r + dh <= height]
            left = jnp.concatenate([lhs(f0, nf, r + dh) for dh in taps], axis=1)
            right = wv[taps[0]:taps[-1] + 1].reshape(len(taps) * 3 * chans, 3 * chans)
            total = jnp.dot(left, right, preferred_element_type=F32)
            acc[r, f0:f0 + nf] = total.reshape(nf, width, 3 * chans)

    for copy in loads:
        copy.wait()
    own(frames - 2, 2)
    when(exists(-1, 0), lambda: tm_copy.wait_recv())
    own(0, frames - 2)

    for where, side in ((0, -1), (1, 1)):
        when(exists(0, -side), lambda: row_copy(side, 0).wait_recv())
        when(exists(0, -side) & exists(1, 0), lambda: relay_copy(where).start())

    reach = 9 * 16
    r3 = lax.broadcasted_iota(jnp.int32, (3, reach), 0)
    c3 = lax.broadcasted_iota(jnp.int32, (3, reach), 1) % 16
    pick = jnp.where((c3 < 9) & (c3 % 3 == r3), 1.0, 0.0).astype(BF16)
    col = lax.broadcasted_iota(jnp.int32, (depth, reach), 1)
    spread = jnp.zeros((depth, reach), F32)
    for tap in range(27):
        part = jnp.dot(d1[tap], pick, preferred_element_type=F32)
        spread = jnp.where((col // 16 == tap // 3) & (col % 16 // 3 == tap % 3), part, spread)
    w1[...] = spread.astype(BF16)
    for tap in range(27):
        k, dw = tap // 3, tap % 3
        w2[dw * depth2:(dw + 1) * depth2, k * depth:(k + 1) * depth] = d2[tap]
    r16 = lax.broadcasted_iota(jnp.int32, (16, 3), 0)
    c16 = lax.broadcasted_iota(jnp.int32, (16, 3), 1)
    pick16 = jnp.where((r16 < 9) & (r16 % 3 == c16), 1.0, 0.0).astype(BF16)
    rgb16 = lax.dot_general(
        pick16, rgb[...], (((1,), (1,)), ((), ())), preferred_element_type=F32
    ).astype(BF16)

    def first_layer(kind):
        for t in range(frames + 2):
            cells = [
                jnp.concatenate(
                    [grid[kind, t + dt, r:r + 3].reshape(48, width) for dt in range(3)], axis=0
                )
                for r in range(height + 2)
            ]
            out = leaky(
                jnp.dot(w1[...], jnp.concatenate(cells, axis=1), preferred_element_type=F32)
            )
            for r in range(height + 2):
                value = out[:, r * width:(r + 1) * width]
                when_t, when_r = tm * frames + t - 1, band * height + r - 1
                inside = (
                    (when_t >= 0) & (when_t < slabs * frames)
                    & (when_r >= 0) & (when_r < bands * height)
                )
                feat[kind, t, r] = jnp.where(inside, value, 0.0).astype(BF16)

    def second_layer(kind, t):
        cells = [
            jnp.concatenate(
                [feat[kind, t + dt, r:r + 3].reshape(3 * depth, width) for dt in range(3)], axis=0
            )
            for r in range(height)
        ]
        out = jnp.dot(w2[...], jnp.concatenate(cells, axis=1), preferred_element_type=F32)
        result = []
        for r in range(height):
            part = out[:, r * width:(r + 1) * width]
            total = (
                shifted(part[:depth2], 1)
                + part[depth2:2 * depth2]
                + shifted(part[2 * depth2:], -1)
            )
            result.append(leaky(total).astype(BF16))
        return result

    grid_wait(1)
    first_layer(1)
    for t in range(frames):
        for r, value in enumerate(second_layer(1, t)):
            second[t, r] = value

    for where, side in ((0, -1), (1, 1)):
        when(exists(0, -side), lambda: row_copy(side, 1).wait_recv())
        when(exists(0, -side) & exists(-1, 0), lambda: relay_copy(where).wait_recv())
    for r, dh, row_in in ((0, 0, 0), (height - 1, 2, height + 1)):
        total = jnp.dot(
            lhs(0, frames, row_in),
            wv[dh].reshape(3 * chans, 3 * chans),
            preferred_element_type=F32,
        )
        acc[r] = acc[r] + total.reshape(frames, width, 3 * chans)

    line = lax.broadcasted_iota(jnp.int32, (width, chans), 0)
    for r in range(height):
        for f in range(frames):
            before = pltpu.roll(acc[r, f, :, 0:chans], 1, 0)
            after = pltpu.roll(acc[r, f, :, 2 * chans:3 * chans], width - 1, 0)
            conv = (
                jnp.where(line == 0, 0.0, before)
                + acc[r, f, :, chans:2 * chans]
                + jnp.where(line == width - 1, 0.0, after)
            )
            value = (lat[f, r].astype(F32) + conv).astype(BF16)
            dec[f, r] = value
            colour = lax.dot_general(
                rgb16, value, (((1,), (1,)), ((), ())), preferred_element_type=F32
            )
            grid[0, f + 2, r + 2] = tripled(colour.astype(BF16).astype(F32))
    grid_send(0)
    grid_wait(0)
    first_layer(0)
    for t in range(frames):
        for r, value in enumerate(second_layer(0, t)):
            near = jnp.abs(feat[0, t + 1, r + 1].astype(F32) - feat[1, t + 1, r + 1].astype(F32))
            far = jnp.abs(value.astype(F32) - second[t, r].astype(F32))
            match[t, r:r + 1] = (
                jnp.sum(near, axis=0, keepdims=True) / depth
                + jnp.sum(far, axis=0, keepdims=True) / depth2
            )

    when(exists(1, 0), lambda: tm_copy.wait_send())
    for where, side in ((0, -1), (1, 1)):
        for half in (0, 1):
            when(exists(0, side), lambda: row_copy(side, half).wait_send())
        when(exists(0, -side) & exists(1, 0), lambda: relay_copy(where).wait_send())
    for kind in (0, 1):
        for side in range(len(SIDES)):
            when(exists(*SIDES[side]), lambda: grid_copy(kind, side).wait_send())


def per_device(
    slabs, bands, latent_feat, norm_gain, conv_weight, rgb_weight, real_frames, disc_first, disc_second
):
    frames, height, width, chans = latent_feat.shape
    depth, depth2 = disc_first.shape[1], disc_second.shape[1]
    vmem = pl.BlockSpec(memory_space=pltpu.VMEM)
    dma = pltpu.SemaphoreType.DMA
    return pl.pallas_call(
        functools.partial(kernel, slabs, bands),
        out_shape=(
            jax.ShapeDtypeStruct(latent_feat.shape, BF16),
            jax.ShapeDtypeStruct((frames, height, width), F32),
        ),
        in_specs=[vmem, vmem, pl.BlockSpec(memory_space=pl.ANY), vmem, vmem, vmem, vmem],
        out_specs=(vmem, vmem),
        scratch_shapes=[
            pltpu.VMEM((3, 3, chans, 3 * chans), BF16),
            pltpu.VMEM((frames + 2, height + 2, width, chans), BF16),
            pltpu.VMEM((height, frames, width, 3 * chans), F32),
            pltpu.VMEM((2, frames + 4, height + 4, 16, width), BF16),
            pltpu.VMEM((2, frames + 2, height + 2, depth, width), BF16),
            pltpu.VMEM((frames, height, depth2, width), BF16),
            pltpu.VMEM((depth, 9 * 16), BF16),
            pltpu.VMEM((3 * depth2, 9 * depth), BF16),
            pltpu.VMEM(real_frames.shape, F32),
            dma((3, 3)),
            dma((2, 2)),
            dma((2, 2)),
            dma,
            dma,
            dma((2,)),
            dma((2,)),
            dma((2, 8)),
            dma((2, 8)),
        ],
        compiler_params=pltpu.CompilerParams(
            collective_id=0, has_side_effects=True, vmem_limit_bytes=48 * 1024 * 1024
        ),
    )(
        latent_feat,
        norm_gain.reshape(1, chans),
        conv_weight.reshape(3, 3, 3, chans, chans),
        rgb_weight,
        real_frames,
        disc_first,
        disc_second,
    )


def solution(mesh):
    placed = (P("tm", "rows", None, None), P(), P(), P(), P(None, "tm", "rows", None), P(), P())
    return jax.shard_map(
        functools.partial(per_device, mesh.shape["tm"], mesh.shape["rows"]),
        mesh=mesh,
        in_specs=placed,
        out_specs=(P("tm", "rows", None, None), P("tm", "rows", None)),
        check_vma=False,
    )
```

```python
import functools

import jax
import jax.numpy as jnp
from jax import lax
from jax.experimental import pallas as pl
from jax.experimental.pallas import tpu as pltpu
from jax.sharding import PartitionSpec as P

MESH = pl.DeviceIdType.MESH
F32 = jnp.float32
BF16 = jnp.bfloat16
SIDES = [(i, j) for i in (-1, 0, 1) for j in (-1, 0, 1) if (i, j) != (0, 0)]


def leaky(value):
    return jnp.maximum(value, 0.2 * value)


def span(step, size):
    if step == 0:
        return 2, 2, size
    return (size, 0, 2) if step > 0 else (2, size + 2, 2)


def shifted(value, step):
    width = value.shape[-1]
    lane = lax.broadcasted_iota(jnp.int32, value.shape, value.ndim - 1)
    moved = pltpu.roll(value, step % width, value.ndim - 1)
    edge = 0 if step > 0 else width - 1
    return jnp.where(lane == edge, 0.0, moved)


def tripled(value):
    row = lax.broadcasted_iota(jnp.int32, value.shape, 0)
    out = jnp.where(row < 3, shifted(value, 1), jnp.where(row < 6, value, shifted(value, -1)))
    return jnp.where(row < 9, out, 0.0).astype(BF16)


def kernel(
    slabs, bands, lat_in, gain_in, w_hbm, rgb_in, real_in, d1_in, d2_in, dec, match,
    lat, gain, rgb, real, d1, d2,
    wv, ext, acc, grid, feat, second, w1, w2, real32,
    in_sem, d2_sem, w_sem, row_s, row_r, tm_s, tm_r, relay_s, relay_r, g_s, g_r,
):
    frames, height, width, chans = lat.shape
    depth, depth2 = d1.shape[2], d2.shape[1] // 3
    tm, band = lax.axis_index("tm"), lax.axis_index("rows")

    def exists(i, j):
        ok = jnp.bool_(True)
        if i:
            ok = ok & (tm + i >= 0) & (tm + i < slabs)
        if j:
            ok = ok & (band + j >= 0) & (band + j < bands)
        return ok

    barrier = pltpu.get_barrier_semaphore()
    count = jnp.int32(0)
    for i, j in SIDES:
        ok = exists(i, j)
        count = count + ok.astype(jnp.int32)

        @pl.when(ok)
        def _(i=i, j=j):
            pl.semaphore_signal(barrier, inc=1, device_id=(tm + i, band + j), device_id_type=MESH)

    inputs = [(lat_in, lat), (gain_in, gain), (real_in, real), (rgb_in, rgb), (d1_in, d1)]
    inputs = [pltpu.make_async_copy(a, b, in_sem.at[i]) for i, (a, b) in enumerate(inputs)]
    for dw in range(3):
        for k in range(9):
            inputs.append(
                pltpu.make_async_copy(
                    d2_in.at[k, dw],
                    d2.at[pl.ds(k * depth, depth), pl.ds(dw * depth2, depth2)],
                    d2_sem.at[k, dw],
                )
            )
    for copy in inputs[:2]:
        copy.start()
    loads = []
    for dh in range(3):
        for dw in range(3):
            copy = pltpu.make_async_copy(
                w_hbm.at[:, dh, dw], wv.at[dh, :, :, pl.ds(dw * chans, chans)], w_sem.at[dh, dw]
            )
            copy.start()
            loads.append(copy)
    for copy in inputs[2:]:
        copy.start()

    inputs[0].wait()
    inputs[1].wait()
    gains = gain[...].reshape(1, chans)
    for f in range(frames):
        for r in range(height):
            x = lat[f, r].astype(F32)
            scale = lax.rsqrt(jnp.mean(x * x, axis=-1, keepdims=True) + 1e-06)
            ext[f + 2, r + 1] = jax.nn.silu(x * scale * gains).astype(BF16)

    @pl.when(tm == 0)
    def _():
        ext[0:2] = jnp.zeros((2,) + ext.shape[1:], BF16)

    @pl.when((band == 0) & (tm > 0))
    def _():
        ext[0:2, 0] = jnp.zeros((2, width, chans), BF16)

    @pl.when((band == bands - 1) & (tm > 0))
    def _():
        ext[0:2, height + 1] = jnp.zeros((2, width, chans), BF16)

    @pl.when(band == 0)
    def _():
        ext[2:, 0] = jnp.zeros((frames, width, chans), BF16)

    @pl.when(band == bands - 1)
    def _():
        ext[2:, height + 1] = jnp.zeros((frames, width, chans), BF16)

    pl.semaphore_wait(barrier, count)

    halves = [(frames, 2), (2, frames - 2)]

    def row_copy(side, half):
        start, size = halves[half]
        mine, theirs = (1, height + 1) if side < 0 else (height, 0)
        where = 0 if side < 0 else 1
        return pltpu.make_async_remote_copy(
            src_ref=ext.at[pl.ds(start, size), mine],
            dst_ref=ext.at[pl.ds(start, size), theirs],
            send_sem=row_s.at[where, half],
            recv_sem=row_r.at[where, half],
            device_id=(tm, band + side),
            device_id_type=MESH,
        )

    tm_copy = pltpu.make_async_remote_copy(
        src_ref=ext.at[pl.ds(frames, 2), pl.ds(1, height)],
        dst_ref=ext.at[pl.ds(0, 2), pl.ds(1, height)],
        send_sem=tm_s,
        recv_sem=tm_r,
        device_id=(tm + 1, band),
        device_id_type=MESH,
    )

    def relay_copy(where):
        row = 0 if where else height + 1
        return pltpu.make_async_remote_copy(
            src_ref=ext.at[pl.ds(frames, 2), row],
            dst_ref=ext.at[pl.ds(0, 2), row],
            send_sem=relay_s.at[where],
            recv_sem=relay_r.at[where],
            device_id=(tm + 1, band),
            device_id_type=MESH,
        )

    def grid_copy(kind, side):
        i, j = SIDES[side]
        (fs, fd, fn), (rs, rd, rn) = span(i, frames), span(j, height)
        return pltpu.make_async_remote_copy(
            src_ref=grid.at[kind, pl.ds(fs, fn), pl.ds(rs, rn)],
            dst_ref=grid.at[kind, pl.ds(fd, fn), pl.ds(rd, rn)],
            send_sem=g_s.at[kind, side],
            recv_sem=g_r.at[kind, side],
            device_id=(tm + i, band + j),
            device_id_type=MESH,
        )

    def when(ok, action):
        pl.when(ok)(action)

    when(exists(1, 0), lambda: tm_copy.start())
    for half in (0, 1):
        for side in (-1, 1):
            when(exists(0, side), lambda: row_copy(side, half).start())

    def grid_zero(kind):
        for side in range(len(SIDES)):
            i, j = SIDES[side]
            (_, fd, fn), (_, rd, rn) = span(i, frames), span(j, height)

            @pl.when(jnp.logical_not(exists(-i, -j)))
            def _():
                grid[kind, fd:fd + fn, rd:rd + rn] = jnp.zeros((fn, rn, 16, width), BF16)

    def grid_send(kind):
        for side in range(len(SIDES)):
            when(exists(*SIDES[side]), lambda: grid_copy(kind, side).start())

    def grid_wait(kind):
        for side in range(len(SIDES)):
            i, j = SIDES[side]
            when(exists(-i, -j), lambda: grid_copy(kind, side).wait_recv())

    grid_zero(0)
    grid_zero(1)
    inputs[2].wait()
    real32[...] = real[...].astype(F32)
    row = lax.broadcasted_iota(jnp.int32, (16, width), 0)
    for f in range(frames):
        for r in range(height):
            b0, b1, b2 = [
                jnp.broadcast_to(real32[c, f, r:r + 1], (16, width)) for c in range(3)
            ]
            cell = jnp.where(row % 3 == 0, b0, jnp.where(row % 3 == 1, b1, b2))
            grid[1, f + 2, r + 2] = tripled(cell)
    grid_send(1)

    def lhs(f0, nf, row):
        return jnp.concatenate(
            [ext[f0 + dt:f0 + dt + nf, row].reshape(nf * width, chans) for dt in range(3)], axis=1
        )

    def own(f0, nf):
        for r in range(height):
            taps = [dh for dh in range(3) if 1 <= r + dh <= height]
            left = jnp.concatenate([lhs(f0, nf, r + dh) for dh in taps], axis=1)
            right = wv[taps[0]:taps[-1] + 1].reshape(len(taps) * 3 * chans, 3 * chans)
            total = jnp.dot(left, right, preferred_element_type=F32)
            acc[r, f0:f0 + nf] = total.reshape(nf, width, 3 * chans)

    for copy in loads:
        copy.wait()
    own(frames - 2, 2)
    when(exists(-1, 0), lambda: tm_copy.wait_recv())
    own(0, frames - 2)

    for where, side in ((0, -1), (1, 1)):
        when(exists(0, -side), lambda: row_copy(side, 0).wait_recv())
        when(exists(0, -side) & exists(1, 0), lambda: relay_copy(where).start())

    for copy in inputs[3:]:
        copy.wait()
    reach = 9 * 16
    tap = lax.broadcasted_iota(jnp.int32, (27, reach), 0)
    col = lax.broadcasted_iota(jnp.int32, (27, reach), 1)
    spread = jnp.zeros((depth, reach), F32)
    for c in range(3):
        pick = (col // 16 == tap // 3) & (col % 16 == tap % 3 * 3 + c)
        spread = spread + lax.dot_general(
            d1[c],
            jnp.where(pick, 1.0, 0.0).astype(BF16),
            (((0,), (0,)), ((), ())),
            preferred_element_type=F32,
        )
    w1[...] = spread.astype(BF16)
    w2[...] = d2[...].T
    r16 = lax.broadcasted_iota(jnp.int32, (16, 3), 0)
    c16 = lax.broadcasted_iota(jnp.int32, (16, 3), 1)
    pick16 = jnp.where((r16 < 9) & (r16 % 3 == c16), 1.0, 0.0).astype(BF16)
    rgb16 = jnp.dot(pick16, rgb[...], preferred_element_type=F32).astype(BF16)

    def first_layer(kind):
        for t in range(frames + 2):
            cells = [
                jnp.concatenate(
                    [grid[kind, t + dt, r:r + 3].reshape(48, width) for dt in range(3)], axis=0
                )
                for r in range(height + 2)
            ]
            out = leaky(
                jnp.dot(w1[...], jnp.concatenate(cells, axis=1), preferred_element_type=F32)
            )
            for r in range(height + 2):
                value = out[:, r * width:(r + 1) * width]
                when_t, when_r = tm * frames + t - 1, band * height + r - 1
                inside = (
                    (when_t >= 0) & (when_t < slabs * frames)
                    & (when_r >= 0) & (when_r < bands * height)
                )
                feat[kind, t, r] = jnp.where(inside, value, 0.0).astype(BF16)

    def second_layer(kind, t):
        cells = [
            jnp.concatenate(
                [feat[kind, t + dt, r:r + 3].reshape(3 * depth, width) for dt in range(3)], axis=0
            )
            for r in range(height)
        ]
        out = jnp.dot(w2[...], jnp.concatenate(cells, axis=1), preferred_element_type=F32)
        result = []
        for r in range(height):
            taps = out[:, r * width:(r + 1) * width]
            total = (
                shifted(taps[:depth2], 1)
                + taps[depth2:2 * depth2]
                + shifted(taps[2 * depth2:], -1)
            )
            result.append(leaky(total).astype(BF16))
        return result

    grid_wait(1)
    first_layer(1)
    for t in range(frames):
        for r, value in enumerate(second_layer(1, t)):
            second[t, r] = value

    def halo(early):
        for r, dh, row_in in ((0, 0, 0), (height - 1, 2, height + 1)):
            for dt in range(3):
                pairs = [(t, t + dt) for t in range(frames)]
                pairs = [(t, f) for t, f in pairs if (2 <= f < frames) != early]
                left = jnp.concatenate([ext[f, row_in] for _, f in pairs], axis=0)
                total = jnp.dot(left, wv[dh, dt], preferred_element_type=F32)
                for n, (t, _) in enumerate(pairs):
                    acc[r, t] = acc[r, t] + total[n * width:(n + 1) * width]

    for where, side in ((0, -1), (1, 1)):
        when(exists(0, -side) & exists(-1, 0), lambda: relay_copy(where).wait_recv())
    halo(True)
    for where, side in ((0, -1), (1, 1)):
        when(exists(0, -side), lambda: row_copy(side, 1).wait_recv())
    halo(False)

    line = lax.broadcasted_iota(jnp.int32, (width, chans), 0)
    for r in range(height):
        for f in range(frames):
            before = pltpu.roll(acc[r, f, :, 0:chans], 1, 0)
            after = pltpu.roll(acc[r, f, :, 2 * chans:3 * chans], width - 1, 0)
            conv = (
                jnp.where(line == 0, 0.0, before)
                + acc[r, f, :, chans:2 * chans]
                + jnp.where(line == width - 1, 0.0, after)
            )
            value = (lat[f, r].astype(F32) + conv).astype(BF16)
            dec[f, r] = value
            colour = lax.dot_general(
                rgb16, value, (((1,), (1,)), ((), ())), preferred_element_type=F32
            )
            grid[0, f + 2, r + 2] = tripled(colour.astype(BF16).astype(F32))
    grid_send(0)
    grid_wait(0)
    first_layer(0)
    for t in range(frames):
        for r, value in enumerate(second_layer(0, t)):
            near = jnp.abs(feat[0, t + 1, r + 1].astype(F32) - feat[1, t + 1, r + 1].astype(F32))
            far = jnp.abs(value.astype(F32) - second[t, r].astype(F32))
            match[t, r:r + 1] = (
                jnp.sum(near, axis=0, keepdims=True) / depth
                + jnp.sum(far, axis=0, keepdims=True) / depth2
            )

    when(exists(1, 0), lambda: tm_copy.wait_send())
    for where, side in ((0, -1), (1, 1)):
        for half in (0, 1):
            when(exists(0, side), lambda: row_copy(side, half).wait_send())
        when(exists(0, -side) & exists(1, 0), lambda: relay_copy(where).wait_send())
    for kind in (0, 1):
        for side in range(len(SIDES)):
            when(exists(*SIDES[side]), lambda: grid_copy(kind, side).wait_send())


def per_device(
    slabs, bands, latent_feat, norm_gain, conv_weight, rgb_weight, real_frames, disc_first, disc_second
):
    frames, height, width, chans = latent_feat.shape
    depth, depth2 = disc_first.shape[1], disc_second.shape[1]
    vmem = pl.BlockSpec(memory_space=pltpu.VMEM)
    dma = pltpu.SemaphoreType.DMA
    return pl.pallas_call(
        functools.partial(kernel, slabs, bands),
        out_shape=(
            jax.ShapeDtypeStruct(latent_feat.shape, BF16),
            jax.ShapeDtypeStruct((frames, height, width), F32),
        ),
        in_specs=[pl.BlockSpec(memory_space=pltpu.HBM)] * 7,
        out_specs=(vmem, vmem),
        scratch_shapes=[
            pltpu.VMEM(latent_feat.shape, BF16),
            pltpu.VMEM(norm_gain.shape, F32),
            pltpu.VMEM((3, chans), BF16),
            pltpu.VMEM(real_frames.shape, BF16),
            pltpu.VMEM((3, 27, depth), BF16),
            pltpu.VMEM((9 * depth, 3 * depth2), BF16),
            pltpu.VMEM((3, 3, chans, 3 * chans), BF16),
            pltpu.VMEM((frames + 2, height + 2, width, chans), BF16),
            pltpu.VMEM((height, frames, width, 3 * chans), F32),
            pltpu.VMEM((2, frames + 4, height + 4, 16, width), BF16),
            pltpu.VMEM((2, frames + 2, height + 2, depth, width), BF16),
            pltpu.VMEM((frames, height, depth2, width), BF16),
            pltpu.VMEM((depth, 9 * 16), BF16),
            pltpu.VMEM((3 * depth2, 9 * depth), BF16),
            pltpu.VMEM(real_frames.shape, F32),
            dma((5,)),
            dma((9, 3)),
            dma((3, 3)),
            dma((2, 2)),
            dma((2, 2)),
            dma,
            dma,
            dma((2,)),
            dma((2,)),
            dma((2, 8)),
            dma((2, 8)),
        ],
        compiler_params=pltpu.CompilerParams(
            collective_id=0, has_side_effects=True, vmem_limit_bytes=61 * 1024 * 1024
        ),
    )(
        latent_feat,
        norm_gain,
        conv_weight.reshape(3, 3, 3, chans, chans),
        rgb_weight.T,
        real_frames,
        jnp.transpose(disc_first, (2, 0, 1)),
        jnp.transpose(disc_second, (0, 2, 1)).reshape(9, 3, depth, depth2),
    )


def solution(mesh):
    placed = (P("tm", "rows", None, None), P(), P(), P(), P(None, "tm", "rows", None), P(), P())
    return jax.shard_map(
        functools.partial(per_device, mesh.shape["tm"], mesh.shape["rows"]),
        mesh=mesh,
        in_specs=placed,
        out_specs=(P("tm", "rows", None, None), P("tm", "rows", None)),
        check_vma=False,
    )
```
